128 devices in a mesh: grp: 4 (over x), ep: 32 (over z, y, core).
Axes of the slice: x: 4, y: 4, z: 4, core: 2. Of those that a mesh axis runs over, the one named last changes fastest.
Arguments:
- layer_input: bfloat16 [16384, 3584], P(('grp', 'ep')), may hold values from -36 to 36
- middle: bfloat16 [16384, 3584], P(('grp', 'ep')), may hold values from -36 to 36
- upstream: bfloat16 [16384, 3584], P(('grp', 'ep')), may hold values from -6 to 6
- gains: float32 [2, 3584], replicated, may hold values from 0.1 to 1.9
- routes: int32 [2, 16384, 1], P(None, ('grp', 'ep')), may hold values from 0 to 31; in each aligned block of 128 rows (0 to 127, 128 to 255, ..., all dimensions but the last counted through in order) at most 6 rows name the same one
- gates: float32 [2, 16384, 1], P(None, ('grp', 'ep')), may hold values from 0.2 to 1
- placement: int32 [2, 32], replicated, may hold values from 0 to 31, each once within a row
- in_proj: bfloat16 [2, 32, 2, 3584, 1024], P(None, 'ep', None, 'grp'), may hold values from -0.09375 to 0.09375
- out_proj: bfloat16 [2, 32, 1024, 3584], P(None, 'ep', None, 'grp'), may hold values from -0.1875 to 0.1875
Outputs:
- grad_input: bfloat16 [16384, 3584], P(('grp', 'ep'))
- grad_in_proj: bfloat16 [2, 32, 2, 3584, 1024], P(None, 'ep', None, 'grp')
- grad_out_proj: bfloat16 [2, 32, 1024, 3584], P(None, 'ep', None, 'grp')
- grad_gains: float32 [2, 3584], replicated
The draws below stay inside these ranges and needn't reach their ends.
Inputs may be any that keep to these rules, and one draw needn't show every extreme that they name: `routes`: in each layer, among the 128 tokens of one device no expert is named by more than 6 tokens, a bound that some block reaches. `placement`: each row names every ep index once.
All inputs are finite; a program needn't handle non-finite values.
Results may differ from the reference program's by a relative error of at most 0.03.
Values may be sent and summed in bfloat16 or wider, within the bound.
No kernel may reach another device: no remote copies, remote signals or barrier semaphores. Data moves between devices by JAX's collectives and lax.ppermute only.
A program may use at most 128 MiB of HBM per device.

```python
import math
import jax
import jax.numpy as jnp
import numpy as np
from jax import lax

D = 3584
FF = 1024
TOK_DEV = 128
TOP = 1
EXPERTS = 32
CAP = 6
TOKENS = 16384
N_GRP = 4
N_EP = 32


def spread_scales(key):
    first_key, second_key = jax.random.split(key)
    low_end = math.log(0.3)
    high_end = math.log(3.0)
    row_scale = jnp.exp(jax.random.uniform(first_key, (TOKENS, 1), jnp.float32, low_end, high_end))
    col_scale = jnp.exp(jax.random.uniform(second_key, (1, D), jnp.float32, low_end, high_end))
    return row_scale * col_scale


def draw_layer_input(key, part):
    key = jax.random.fold_in(key, 11)
    noise_key, scale_key = jax.random.split(key, 2)
    noise = jax.random.truncated_normal(noise_key, -4.0, 4.0, (TOKENS, D), jnp.float32)
    return (noise * spread_scales(scale_key)).astype(jnp.bfloat16)


def draw_middle(key, part):
    key = jax.random.fold_in(key, 12)
    noise_key, scale_key = jax.random.split(key, 2)
    noise = jax.random.truncated_normal(noise_key, -4.0, 4.0, (TOKENS, D), jnp.float32)
    return (noise * spread_scales(scale_key)).astype(jnp.bfloat16)


def block_levels(own_key, extent, shards, smallest, high):
    def one(position, blocks):
        draws = jax.random.uniform(jax.random.fold_in(jax.random.fold_in(own_key, 6), position), (blocks,), jnp.float32, smallest / len(shards), high / len(shards))
        return jnp.repeat(jnp.exp(draws), extent[position] // blocks).reshape((-1,) + (1,) * (len(extent) - position - 1))

    level = one(*shards[0])
    for cut in shards[1:]:
        level = level * one(*cut)
    return level


def shared_out(own_key, own, number, rows, count, top, limit, skew):
    sequence = jax.random.permutation(own_key, count)
    packed, usual = shares(count, rows * top, limit, skew, True), shares(count, rows * top, limit, skew, False)
    places = jnp.arange(count)

    def named(tallies, offset_by):
        used = int((tallies > 0).sum())
        fixed = max(1, used // 4)
        moved = fixed + (places - fixed + offset_by * (used - fixed)) % max(1, count - fixed)
        return jnp.zeros((count,), jnp.int32).at[sequence[jnp.where(places < fixed, places, moved)]].set(jnp.asarray(tallies, jnp.int32))

    tallies = jnp.where(number % 4 == 0, named(packed, number // 4), named(usual, number - number // 4 - 1))
    mixed = jax.random.permutation(jax.random.fold_in(own, 3), count)
    source_of, taker = mixed[0:count // 2 * 2:2], mixed[1:count // 2 * 2:2]
    room = jnp.minimum(tallies[source_of] - 1, limit - tallies[taker]) // 2
    room = jnp.where((source_of == sequence[0]) | (taker == sequence[0]) | (tallies[taker] == 0), 0, jnp.maximum(room, 0))
    moved = jax.random.randint(jax.random.fold_in(own, 4), (count // 2,), 0, 1 << 20) % (room + 1)
    tallies = tallies.at[source_of].add(-moved).at[taker].add(moved)
    items = jnp.searchsorted(jnp.cumsum(tallies), jnp.arange(rows * top), side="right").astype(jnp.int32)
    listing = items.reshape(top, rows).T
    listing = listing[jax.random.permutation(jax.random.fold_in(own, 1), rows)]
    offset_by = jax.random.randint(jax.random.fold_in(own, 2), (rows, 1), 0, top)
    return jnp.take_along_axis(listing, (jnp.arange(top)[None, :] + offset_by) % top, axis=1)


def shares(number_of, total, bound, slope, full):
    portions = [(1 << 20) // math.isqrt(grade ** slope) + 1 for grade in range(1, number_of + 1)]
    largest = bound if full else min(bound, max(-(-total // number_of), total * portions[0] // sum(portions)))
    least = 1 if total - largest >= number_of - 1 else 0
    given, surplus = [largest] + [least] * (number_of - 1), total - largest - least * (number_of - 1)
    while surplus > 0:
        movable = [i for i in range(1, number_of) if given[i] < largest] or [i for i in range(1, number_of) if given[i] < bound]
        mass, remaining = sum([portions[i] for i in movable]), surplus
        for i in movable:
            addition = min(bound - given[i], max(1, remaining * portions[i] // mass), surplus)
            given[i] = given[i] + addition
            surplus = surplus - addition
    return np.array(given)


def normal_values(rng, dims, spread, bound, pieces=(), held_as=jnp.bfloat16):
    entries = jax.random.normal(rng, dims, jnp.float32) * spread
    if len(pieces) > 0:
        entries = block_levels(rng, dims, pieces, -0.22, 0.18) * entries
    return jnp.clip(entries, min=-bound, max=bound).astype(held_as)


def setup_inputs(seed: int = 0) -> dict:
    splits = jax.random.split(jax.random.key(seed), 10)
    layer_input = draw_layer_input(jax.random.fold_in(splits[9], 71), 0)
    middle = draw_middle(jax.random.fold_in(splits[9], 71), 0)
    upstream = normal_values(splits[2], (TOKENS, D), 1.0, 6.0, ((0, 128),))
    gains = jnp.clip(1.0 + 0.18 * jax.random.normal(splits[3], (2, D), jnp.float32), 0.1, 1.9)
    routes_keys = jax.random.split(jax.random.fold_in(splits[4], 1), 2 * TOKENS // TOK_DEV)
    routes_turns = jax.random.permutation(jax.random.fold_in(splits[4], 3), 2 * TOKENS // TOK_DEV)
    routes = jax.vmap(lambda own, number: shared_out(jax.random.fold_in(splits[4], 2), own, number, TOK_DEV, EXPERTS, TOP, CAP, 1))(routes_keys, routes_turns).reshape((2, TOKENS, TOP))
    gates = jnp.clip(0.2 + 0.8 * jax.random.uniform(splits[5], (2, TOKENS, TOP), jnp.float32) ** block_levels(splits[5], (2, TOKENS, TOP), ((1, 128),), -0.2, 0.2), 0.2, 1.0)
    placement = jax.vmap(lambda own: jax.random.permutation(own, EXPERTS))(jax.random.split(splits[6], 2)).reshape((2, EXPERTS)).astype(jnp.int32)
    in_proj = normal_values(splits[7], (2, EXPERTS, 2, D, FF), D ** -0.5, 0.09375, ((1, 32), (3, 4)))
    out_proj = normal_values(splits[8], (2, EXPERTS, FF, D), FF ** -0.5, 0.1875, ((1, 32), (3, 4)))
    return dict(layer_input=layer_input, middle=middle, upstream=upstream, gains=gains, routes=routes, gates=gates, placement=placement, in_proj=in_proj, out_proj=out_proj)


def norm_parts(activation, gain_row):
    widened = activation.astype(jnp.float32)
    inverse = lax.rsqrt(lax.optimization_barrier(jnp.mean(widened * widened, axis=-1, keepdims=True)) + 1e-06)
    unit_feat = widened * inverse
    return (inverse, unit_feat, (unit_feat * gain_row).astype(jnp.bfloat16))

def block_sums(row_block, weight_blocks, form):
    row_count = row_block.shape[0]
    split_rows = row_block.astype(jnp.float32).reshape(row_count, N_GRP, D // N_GRP)
    partial_value = jnp.einsum(form, split_rows, weight_blocks.astype(jnp.float32))
    rounded = lax.optimization_barrier(partial_value.astype(jnp.bfloat16))
    return lax.optimization_barrier(jnp.sum(rounded.astype(jnp.float32), axis=1))

def unit_grads(pre_gate, pre_up, back_hidden):
    sigmoid_gate = jax.nn.sigmoid(pre_gate)
    active = pre_gate * sigmoid_gate
    hidden = (active * pre_up).astype(jnp.bfloat16)
    d_gate = (back_hidden * pre_up * sigmoid_gate * (1.0 + pre_gate * (1.0 - sigmoid_gate))).astype(jnp.bfloat16)
    d_up = (back_hidden * active).astype(jnp.bfloat16)
    return (hidden, d_gate, d_up)

def expert_back(normed_rows, scaled_rows, w_gate, w_up, w_down):
    gate_blocks = w_gate.reshape(N_GRP, D // N_GRP, FF)
    up_blocks = w_up.reshape(N_GRP, D // N_GRP, FF)
    down_blocks = w_down.reshape(FF, N_GRP, D // N_GRP)
    pre_gate = block_sums(normed_rows, gate_blocks, 'rgq,gqf->rgf')
    pre_up = block_sums(normed_rows, up_blocks, 'rgq,gqf->rgf')
    back_hidden = block_sums(scaled_rows, down_blocks, 'rgq,fgq->rgf')
    hidden, d_gate, d_up = unit_grads(pre_gate, pre_up, back_hidden)
    d_rows = jnp.dot(d_gate, w_gate.T, preferred_element_type=jnp.float32)
    d_rows = (d_rows + jnp.dot(d_up, w_up.T, preferred_element_type=jnp.float32)).astype(jnp.bfloat16)
    grad_gate = jnp.dot(normed_rows.T, d_gate, preferred_element_type=jnp.float32).astype(jnp.bfloat16)
    grad_up = jnp.dot(normed_rows.T, d_up, preferred_element_type=jnp.float32).astype(jnp.bfloat16)
    grad_down = jnp.dot(hidden.T, scaled_rows, preferred_element_type=jnp.float32).astype(jnp.bfloat16)
    return (d_rows, grad_gate, grad_up, grad_down)

def layer_back(activation, grad_above, gain_row, route_rows, gate_rows, place_row, in_layer, out_layer):
    inverse, unit_feat, normed = norm_parts(activation, gain_row)
    expert_ids = jnp.arange(EXPERTS, dtype=jnp.int32)
    expert_hit = route_rows[:, 0][:, None] == expert_ids[None, :]
    target = lax.optimization_barrier(jnp.sum(jnp.where(expert_hit, place_row[None, :], 0), axis=1)).astype(jnp.int32)
    scaled = (gate_rows[:, 0:1] * grad_above.astype(jnp.float32)).astype(jnp.bfloat16)
    sorted_tokens = jnp.argsort(target, stable=True).astype(jnp.int32)
    counts = lax.optimization_barrier(jnp.sum((target[:, None] == expert_ids[None, :]).astype(jnp.int32), axis=0))
    starts = (jnp.cumsum(counts) - counts).astype(jnp.int32)
    row_limit = N_GRP * N_EP * CAP
    padded = jnp.concatenate([sorted_tokens, jnp.zeros((row_limit,), jnp.int32)])

    def per_slot(slot_id):
        row_index = lax.dynamic_slice(padded, (starts[slot_id],), (row_limit,))
        valid_row = (jnp.arange(row_limit, dtype=jnp.int32) < counts[slot_id])[:, None]
        picked = jnp.where(valid_row, normed[row_index], jnp.zeros((), jnp.bfloat16))
        picked_up = jnp.where(valid_row, scaled[row_index], jnp.zeros((), jnp.bfloat16))
        results = expert_back(picked, picked_up, in_layer[slot_id, 0], in_layer[slot_id, 1], out_layer[slot_id])
        return (row_index,) + results
    row_index, d_rows, grad_gate, grad_up, grad_down = lax.map(per_slot, expert_ids)
    d_normed = jnp.zeros((TOKENS, D), jnp.float32).at[row_index.reshape(-1)].add(d_rows.reshape(-1, D).astype(jnp.float32))
    d_scaled = d_normed * gain_row
    grad_gain = lax.optimization_barrier(jnp.sum(d_normed * unit_feat, axis=0))
    grad_below = grad_above.astype(jnp.float32) + inverse * (d_scaled - unit_feat * lax.optimization_barrier(jnp.mean(d_scaled * unit_feat, axis=-1, keepdims=True)))
    return (grad_below.astype(jnp.bfloat16), jnp.stack([grad_gate, grad_up], axis=1), grad_down, grad_gain)

def reference(layer_input, middle, upstream, gains, routes, gates, placement, in_proj, out_proj):
    upper_layer = layer_back(middle, upstream, gains[1], routes[1], gates[1], placement[1], in_proj[1], out_proj[1])
    lower_layer = layer_back(layer_input, upper_layer[0], gains[0], routes[0], gates[0], placement[0], in_proj[0], out_proj[0])
    grad_in_proj = jnp.stack([lower_layer[1], upper_layer[1]])
    grad_out_proj = jnp.stack([lower_layer[2], upper_layer[2]])
    grad_gains = jnp.stack([lower_layer[3], upper_layer[3]])
    return (lower_layer[0], grad_in_proj, grad_out_proj, grad_gains)
```

```python
import jax
import jax.numpy as jnp
from jax import lax
from jax.sharding import PartitionSpec as P

f32 = jnp.float32
bf16 = jnp.bfloat16


def shift_grp(array, step):
    groups = lax.axis_size("grp")
    pairs = [(i, (i + step) % groups) for i in range(groups)]
    return lax.ppermute(array, "grp", pairs)


def block_of(array, index, extent, axis):
    return lax.dynamic_slice_in_dim(array, index * extent, extent, axis)


def split_features(array):
    groups = lax.axis_size("grp")
    here = lax.axis_index("grp")
    width = array.shape[1] // groups
    slots = [block_of(array, here, width, 1)]
    for step in range(1, groups):
        slots.append(shift_grp(block_of(array, (here + step) % groups, width, 1), step))
    return jnp.stack(slots).reshape(groups * array.shape[0], width)


def join_features(rows):
    groups = lax.axis_size("grp")
    here = lax.axis_index("grp")
    width = rows.shape[1]
    slots = rows.reshape(groups, -1, width)
    whole = jnp.zeros((slots.shape[1], groups * width), rows.dtype)
    for step in range(groups):
        piece = slots[step] if step == 0 else shift_grp(slots[step], -step)
        whole = lax.dynamic_update_slice(whole, piece, (0, (here + step) % groups * width))
    return whole


def spread_small(array):
    groups = lax.axis_size("grp")
    return jnp.stack([array] + [shift_grp(array, step) for step in range(1, groups)])


def sum_slots(partial):
    groups = lax.axis_size("grp")
    total = partial
    for step in range(1, groups):
        total = total + jnp.roll(shift_grp(partial, step), step, axis=0)
    return total


def scatter_sum(partial):
    groups = lax.axis_size("grp")
    here = lax.axis_index("grp")
    rows = partial.shape[0] // groups
    total = block_of(partial, here, rows, 0).astype(f32)
    for step in range(1, groups):
        piece = block_of(partial, (here + step) % groups, rows, 0)
        total = total + shift_grp(piece, step).astype(f32)
    return total


def gather_rows(quarter):
    groups = lax.axis_size("grp")
    here = lax.axis_index("grp")
    rows = quarter.shape[0]
    whole = jnp.zeros((groups * rows, quarter.shape[1]), quarter.dtype)
    for step in range(groups):
        piece = quarter if step == 0 else shift_grp(quarter, step)
        whole = lax.dynamic_update_slice(whole, piece, ((here - step) % groups * rows, 0))
    return whole


def all_sum(partial):
    return gather_rows(scatter_sum(partial).astype(bf16)).astype(f32)


def to_experts(rows):
    return lax.all_to_all(rows, "ep", split_axis=0, concat_axis=0, tiled=True)


def unit_grads(pre_gate, pre_up, back_hidden):
    sigmoid_gate = jax.nn.sigmoid(pre_gate)
    active = pre_gate * sigmoid_gate
    d_gate = (back_hidden * pre_up * sigmoid_gate * (1.0 + pre_gate * (1.0 - sigmoid_gate))).astype(
        bf16
    )
    d_up = (back_hidden * active).astype(bf16)
    return d_gate, d_up


def hidden_of(pre_gate, pre_up):
    return (pre_gate * jax.nn.sigmoid(pre_gate) * pre_up).astype(bf16)


def rows_grad(d_gate, d_up, w_gate, w_up):
    contract = (((1,), (1,)), ((), ()))
    total = lax.dot_general(d_gate, w_gate, contract, preferred_element_type=f32)
    return total + lax.dot_general(d_up, w_up, contract, preferred_element_type=f32)


def outer_sum(left_rows, right_rows):
    return lax.dot_general(
        left_rows, right_rows, (((0,), (0,)), ((), ())), preferred_element_type=f32
    ).astype(bf16)


def row_target(route_rows, place_row, capacity):
    experts = lax.axis_size("ep")
    expert_ids = jnp.arange(experts, dtype=jnp.int32)
    expert_hit = route_rows[:, 0][:, None] == expert_ids[None, :]
    dest_slot = jnp.sum(jnp.where(expert_hit, place_row[None, :], 0), axis=1)
    slot_hit = (dest_slot[:, None] == expert_ids[None, :]).astype(jnp.int32)
    slot_rank = jnp.sum(jnp.cumsum(slot_hit, axis=0) * slot_hit, axis=1) - 1
    return dest_slot * (lax.axis_size("grp") * capacity) + slot_rank


def inverse_of(activation):
    widened = activation.astype(f32)
    return lax.rsqrt(jnp.mean(widened * widened, axis=-1) + 1e-06)


def picker_of(target, row_total):
    return (jnp.arange(row_total, dtype=jnp.int32)[:, None] == target[None, :]).astype(bf16)


def pick(picker, rows):
    return jnp.dot(picker, rows, preferred_element_type=f32).astype(bf16)


def unpick(picker, rows):
    return lax.dot_general(picker, rows, (((0,), (0,)), ((), ())), preferred_element_type=f32)


def pre_parts(features, w_gate, w_up):
    return (
        jnp.dot(features, w_gate, preferred_element_type=f32).astype(bf16),
        jnp.dot(features, w_up, preferred_element_type=f32).astype(bf16),
    )


def back_part(up_rows, w_down):
    return lax.dot_general(
        up_rows, w_down, (((1,), (1,)), ((), ())), preferred_element_type=f32
    ).astype(bf16)


def below(grad_above, inverse, unit_feat, d_normed, gain_row):
    groups = lax.axis_size("grp")
    width = unit_feat.shape[1]
    d_scaled = d_normed * gain_row
    partial = jnp.sum(d_scaled * unit_feat, axis=-1).reshape(groups, -1)
    mean = sum_slots(partial).reshape(-1, 1) / (groups * width)
    return (grad_above.astype(f32) + inverse * (d_scaled - unit_feat * mean)).astype(bf16)


def sum_ep(array):
    size = lax.axis_size("ep")
    step = 1
    while step < size:
        array = array + lax.ppermute(array, "ep", [(i, i ^ step) for i in range(size)])
        step *= 2
    return array


def body(layer_input, middle, upstream, gains, routes, gates, placement, in_proj, out_proj):
    groups = lax.axis_size("grp")
    experts = lax.axis_size("ep")
    here = lax.axis_index("grp")
    tokens = middle.shape[0]
    width = middle.shape[1] // groups
    capacity = 3 * tokens // (2 * experts)
    row_total = groups * experts * capacity
    gain_block = block_of(gains, here, width, 1)

    middle_t = split_features(middle)
    small = jnp.stack(
        [
            inverse_of(layer_input),
            inverse_of(middle),
            gates[0, :, 0],
            gates[1, :, 0],
            row_target(routes[0], placement[0], capacity).astype(f32),
            row_target(routes[1], placement[1], capacity).astype(f32),
        ]
    )
    small_t = spread_small(small)
    inverse = [small_t[:, j].reshape(-1, 1) for j in range(2)]
    gate = [small_t[:, 2 + j].reshape(-1, 1) for j in range(2)]
    ranks = ((here - jnp.arange(groups, dtype=jnp.int32)) % groups * capacity)[:, None]
    picker = [
        picker_of((small_t[:, 4 + j].astype(jnp.int32) + ranks).reshape(-1), row_total)
        for j in range(2)
    ]

    unit_1 = middle_t.astype(f32) * inverse[1]
    features_1 = to_experts(pick(picker[1], (unit_1 * gain_block[1]).astype(bf16)))
    upstream_t = split_features(upstream)
    scaled_1 = (gate[1] * upstream_t.astype(f32)).astype(bf16)
    up_rows_1 = to_experts(pick(picker[1], scaled_1))
    input_t = split_features(layer_input)
    unit_0 = input_t.astype(f32) * inverse[0]
    features_0 = to_experts(pick(picker[0], (unit_0 * gain_block[0]).astype(bf16)))

    w_gate, w_up, w_down = in_proj[1, 0, 0], in_proj[1, 0, 1], out_proj[1, 0]
    part_gate, part_up = pre_parts(features_1, w_gate, w_up)
    pre_gate, pre_up = scatter_sum(part_gate), scatter_sum(part_up)
    back_hidden = scatter_sum(back_part(up_rows_1, w_down))
    d_gate, d_up = unit_grads(pre_gate, pre_up, back_hidden)
    d_gate, d_up = gather_rows(d_gate), gather_rows(d_up)
    hidden = gather_rows(hidden_of(pre_gate, pre_up))
    d_rows = rows_grad(d_gate, d_up, w_gate, w_up).astype(bf16)
    d_normed = unpick(picker[1], to_experts(d_rows))
    grad_gate_1 = outer_sum(features_1, d_gate)
    grad_up_1 = outer_sum(features_1, d_up)
    grad_down_1 = outer_sum(hidden, up_rows_1)
    gain_part_1 = jnp.sum(d_rows.astype(f32) * features_1.astype(f32), axis=0)

    w_gate, w_up, w_down = in_proj[0, 0, 0], in_proj[0, 0, 1], out_proj[0, 0]
    part_gate, part_up = pre_parts(features_0, w_gate, w_up)
    pre_gate, pre_up = all_sum(part_gate), all_sum(part_up)
    hidden = hidden_of(pre_gate, pre_up)

    grad_mid = below(upstream_t, inverse[1], unit_1, d_normed, gain_block[1])
    scaled_0 = (gate[0] * grad_mid.astype(f32)).astype(bf16)
    up_rows_0 = to_experts(pick(picker[0], scaled_0))
    back_hidden = all_sum(back_part(up_rows_0, w_down))
    d_gate, d_up = unit_grads(pre_gate, pre_up, back_hidden)
    d_rows = rows_grad(d_gate, d_up, w_gate, w_up).astype(bf16)
    d_normed = unpick(picker[0], to_experts(d_rows))
    gain_part_0 = jnp.sum(d_rows.astype(f32) * features_0.astype(f32), axis=0)
    grad_gate_0 = outer_sum(features_0, d_gate)
    grad_up_0 = outer_sum(features_0, d_up)
    grad_down_0 = outer_sum(hidden, up_rows_0)

    gain_sum = sum_ep(jnp.stack([gain_part_0, gain_part_1]) / gain_block)
    grad_gains = jnp.zeros(gains.shape, f32)
    for step in range(groups):
        piece = gain_sum if step == 0 else shift_grp(gain_sum, step)
        grad_gains = lax.dynamic_update_slice(
            grad_gains, piece, (0, (here - step) % groups * width)
        )

    grad_input = join_features(below(grad_mid, inverse[0], unit_0, d_normed, gain_block[0]))
    grad_in_proj = jnp.stack(
        [jnp.stack([grad_gate_0, grad_up_0]), jnp.stack([grad_gate_1, grad_up_1])]
    )[:, None]
    grad_out_proj = jnp.stack([grad_down_0, grad_down_1])[:, None]
    return (grad_input, grad_in_proj, grad_out_proj, grad_gains)


def solution(mesh):
    return jax.shard_map(
        body,
        mesh=mesh,
        in_specs=(
            P(("grp", "ep"), None),
            P(("grp", "ep"), None),
            P(("grp", "ep"), None),
            P(),
            P(None, ("grp", "ep"), None),
            P(None, ("grp", "ep"), None),
            P(),
            P(None, "ep", None, "grp", None),
            P(None, "ep", None, "grp"),
        ),
        out_specs=(
            P(("grp", "ep"), None),
            P(None, "ep", None, "grp", None),
            P(None, "ep", None, "grp"),
            P(),
        ),
        check_vma=False,
    )
```

```python
import jax
import jax.numpy as jnp
from jax import lax
from jax.experimental import pallas as pl
from jax.experimental.pallas import tpu as pltpu
from jax.sharding import PartitionSpec as P

f32 = jnp.float32
bf16 = jnp.bfloat16
LANES = 128


def shift_grp(array, step):
    groups = lax.axis_size("grp")
    pairs = [(i, (i + step) % groups) for i in range(groups)]
    return lax.ppermute(array, "grp", pairs)


def block_of(array, index, extent, axis):
    return lax.dynamic_slice_in_dim(array, index * extent, extent, axis)


def feature_blocks(array):
    groups = lax.axis_size("grp")
    here = lax.axis_index("grp")
    width = array.shape[1] // groups
    return [block_of(array, (here + step) % groups, width, 1) for step in range(groups)]


def send_blocks(blocks):
    return [block if step == 0 else shift_grp(block, step) for step, block in enumerate(blocks)]


def join_features(rows):
    groups = lax.axis_size("grp")
    here = lax.axis_index("grp")
    width = rows.shape[1]
    slots = rows.reshape(groups, -1, width)
    pieces = [slots[0]] + [shift_grp(slots[step], -step) for step in range(1, groups)]
    whole = jnp.zeros((slots.shape[1], groups * width), rows.dtype)
    for step, piece in enumerate(pieces):
        whole = lax.dynamic_update_slice(whole, piece, (0, (here + step) % groups * width))
    return whole, pieces[1]


def spread_small(array):
    groups = lax.axis_size("grp")
    return jnp.stack([array] + [shift_grp(array, step) for step in range(1, groups)])


def after(array, *others):
    return lax.optimization_barrier((array,) + others)[0]


def send_chunks(chunks):
    return [chunk if step == 0 else shift_grp(chunk, step) for step, chunk in enumerate(chunks)]


def scatter_halves(halves):
    own, right, far, left = halves
    from_left, from_right = shift_grp(far[0], 1), shift_grp(far[1], -1)
    left_bottom, right_top = shift_grp(right[1], 1), shift_grp(left[0], -1)
    left_top = shift_grp((right[0].astype(f32) + from_left.astype(f32)).astype(bf16), 1)
    right_bottom = shift_grp((left[1].astype(f32) + from_right.astype(f32)).astype(bf16), -1)
    return (own[0], left_top, right_top), (own[1], left_bottom, right_bottom)


def gather_halves(top, bottom):
    left, right = (shift_grp(top, 1), shift_grp(bottom, 1)), (shift_grp(top, -1), shift_grp(bottom, -1))
    far = shift_grp(left[0], 1), shift_grp(right[1], -1)
    return (top, bottom), right, far, left


def flat(pairs):
    return [half for pair in pairs for half in pair]


def call(kernel, grid_args, out_shapes, flops, scratch=()):
    in_specs = []
    for array, block, index in grid_args:
        shape = array.shape if block is None else block
        place = (0,) * len(shape) if index is None else index
        in_specs.append(pl.BlockSpec(shape, lambda i, here, place=place: place))
    out_specs = [
        pl.BlockSpec(shape.shape, lambda i, here, n=len(shape.shape): (0,) * n)
        for shape in out_shapes
    ]
    moved = sum(array.size * array.dtype.itemsize for array, block, _ in grid_args if block is None)
    moved += sum(shape.size * shape.dtype.itemsize for shape in out_shapes)
    return pl.pallas_call(
        kernel,
        grid_spec=pltpu.PrefetchScalarGridSpec(
            num_scalar_prefetch=1, grid=(1,), in_specs=in_specs, out_specs=out_specs,
            scratch_shapes=scratch,
        ),
        out_shape=out_shapes,
        compiler_params=pltpu.CompilerParams(vmem_limit_bytes=48 * 1024 * 1024),
        cost_estimate=pl.CostEstimate(flops=flops, bytes_accessed=moved, transcendentals=0),
    )(lax.axis_index("grp").reshape(1), *(array for array, _, _ in grid_args))


def nn(left, right):
    return lax.dot_general(left, right, (((1,), (0,)), ((), ())), preferred_element_type=f32)


def nt(left, right):
    return lax.dot_general(left, right, (((1,), (1,)), ((), ())), preferred_element_type=f32)


def rows_at(here, step, rows):
    groups = 4
    return pl.ds(pl.multiple_of((here + step) % groups * rows, 16), rows)


def turn(here, turned, x_ref, rows):
    for step in range(4):
        turned[step * rows : (step + 1) * rows, :] = x_ref[rows_at(here[0], step, rows), :]


def pre_parts(features, in_proj, layer):
    rows, units = features.shape[0] // 4, in_proj.shape[-1]
    half = rows // 2

    def kernel(here, x_ref, w_ref, *refs):
        outs, turned = refs[:8], refs[8]
        turn(here, turned, x_ref, rows)
        for part in range(2):
            whole = nn(turned[...], w_ref[0, 0, part]).astype(bf16)
            for place in range(8):
                outs[place][part] = whole[place * half : (place + 1) * half]

    outs = call(
        kernel,
        [(features, None, None), (in_proj, (1, 1) + in_proj.shape[2:], (layer, 0, 0, 0, 0))],
        [jax.ShapeDtypeStruct((2, half, units), bf16)] * 8,
        4 * features.size * units,
        [pltpu.VMEM(features.shape, bf16)],
    )
    return [outs[2 * step : 2 * step + 2] for step in range(4)]


def back_parts(up_rows, out_proj, layer):
    rows, units = up_rows.shape[0] // 4, out_proj.shape[2]
    half = rows // 2

    def kernel(here, x_ref, w_ref, *refs):
        outs, turned = refs[:8], refs[8]
        turn(here, turned, x_ref, rows)
        whole = nt(turned[...], w_ref[0, 0]).astype(bf16)
        for place in range(8):
            outs[place][...] = whole[place * half : (place + 1) * half]

    outs = call(
        kernel,
        [(up_rows, None, None), (out_proj, (1, 1) + out_proj.shape[2:], (layer, 0, 0, 0))],
        [jax.ShapeDtypeStruct((half, units), bf16)] * 8,
        2 * up_rows.size * units,
        [pltpu.VMEM(up_rows.shape, bf16)],
    )
    return [outs[2 * step : 2 * step + 2] for step in range(4)]


def grads_of(pre_gate, pre_up, back_hidden):
    sigmoid_gate = jax.nn.sigmoid(pre_gate)
    active = pre_gate * sigmoid_gate
    d_gate = back_hidden * pre_up * sigmoid_gate * (1.0 + pre_gate * (1.0 - sigmoid_gate))
    d_gate, d_up = d_gate.astype(bf16), (back_hidden * active).astype(bf16)
    dots = d_gate.astype(f32) * pre_gate + d_up.astype(f32) * pre_up
    dots = jnp.sum(dots, axis=-1, keepdims=True)
    high = dots.astype(bf16).astype(f32)
    lane = lax.broadcasted_iota(jnp.int32, (dots.shape[0], LANES), 1)
    tail = jnp.where(lane == 0, high, jnp.where(lane == 1, dots - high, 0.0)).astype(bf16)
    return (active * pre_up).astype(bf16), d_gate, d_up, tail


def total(refs, *index):
    value = refs[0][index].astype(f32)
    for ref in refs[1:]:
        value = value + ref[index].astype(f32)
    return value


def quarter_grads(pres, backs):
    half, units = backs[0][0].shape

    def kernel(here, *refs):
        for side in range(2):
            pre, back = refs[3 * side : 3 * side + 3], refs[6 + 3 * side : 9 + 3 * side]
            packed, hidden_ref = refs[12 + side], refs[14 + side]
            hidden, d_gate, d_up, tail = grads_of(total(pre, 0), total(pre, 1), total(back, ...))
            packed[:, :units] = d_gate
            packed[:, units : 2 * units] = d_up
            packed[:, 2 * units :] = tail
            hidden_ref[...] = hidden

    packed = jax.ShapeDtypeStruct((half, 2 * units + LANES), bf16)
    hidden = jax.ShapeDtypeStruct((half, units), bf16)
    outs = call(
        kernel,
        [(array, None, None) for array in flat(pres) + flat(backs)],
        [packed, packed, hidden, hidden],
        0,
    )
    return outs[:2], outs[2:]


def sum_parts(parts):
    def kernel(here, *refs):
        for side in range(2):
            refs[6 + side][...] = total(refs[3 * side : 3 * side + 3], ...).astype(bf16)

    return call(
        kernel,
        [(part, None, None) for part in flat(parts)],
        [jax.ShapeDtypeStruct(parts[0][0].shape, bf16)] * 2,
        0,
    )


def places(here, half):
    return [
        pl.ds(pl.multiple_of((here[0] + k // 2) % 4 * (2 * half) + k % 2 * half, 16), half)
        for k in range(8)
    ]


def store_rows(out, width, grads, w_ref):
    d_rows = nt(grads[0], w_ref[0, 0, 0]) + nt(grads[1], w_ref[0, 0, 1])
    out[:, :width] = d_rows.astype(bf16)


def rows_from_grads(pieces, in_proj, layer):
    half, width, units = pieces[0][0].shape[0], in_proj.shape[3], in_proj.shape[4]

    def kernel(here, *refs):
        w_ref, out, grads = refs[8:]
        for piece, at in zip(refs[:8], places(here, half)):
            grads[0, at, :] = piece[:, :units]
            grads[1, at, :] = piece[:, units : 2 * units]
            out[at, width:] = piece[:, 2 * units :]
        store_rows(out, width, grads, w_ref)

    return call(
        kernel,
        [(piece, None, None) for piece in flat(pieces)]
        + [(in_proj, (1, 1) + in_proj.shape[2:], (layer, 0, 0, 0, 0))],
        [
            jax.ShapeDtypeStruct((8 * half, width + LANES), bf16),
            jax.ShapeDtypeStruct((2, 8 * half, units), bf16),
        ],
        32 * half * width * units,
    )


def rows_from_sums(pres, backs, in_proj, layer):
    (half, units), width = backs[0][0].shape, in_proj.shape[3]

    def kernel(here, *refs):
        pre, back, (w_ref, out, grads) = refs[:8], refs[8:16], refs[16:]
        for k, at in enumerate(places(here, half)):
            _, d_gate, d_up, tail = grads_of(
                pre[k][0].astype(f32), pre[k][1].astype(f32), back[k][...].astype(f32)
            )
            grads[0, at, :] = d_gate
            grads[1, at, :] = d_up
            out[at, width:] = tail
        store_rows(out, width, grads, w_ref)

    return call(
        kernel,
        [(array, None, None) for array in flat(pres) + flat(backs)]
        + [(in_proj, (1, 1) + in_proj.shape[2:], (layer, 0, 0, 0, 0))],
        [
            jax.ShapeDtypeStruct((8 * half, width + LANES), bf16),
            jax.ShapeDtypeStruct((2, 8 * half, units), bf16),
        ],
        32 * half * width * units,
    )


def hidden_from_sums(pres):
    _, half, units = pres[0][0].shape

    def kernel(here, *refs):
        for pre, at in zip(refs[:8], places(here, half)):
            gate = pre[0].astype(f32)
            hidden = gate * jax.nn.sigmoid(gate) * pre[1].astype(f32)
            refs[8][at, :] = hidden.astype(bf16)

    return call(
        kernel,
        [(pre, None, None) for pre in flat(pres)],
        [jax.ShapeDtypeStruct((8 * half, units), bf16)],
        0,
    )[0]


def join_rows(pieces):
    half, units = pieces[0][0].shape

    def kernel(here, *refs):
        for piece, at in zip(refs[:8], places(here, half)):
            refs[8][at, :] = piece[...]

    return call(
        kernel,
        [(piece, None, None) for piece in flat(pieces)],
        [jax.ShapeDtypeStruct((8 * half, units), bf16)],
        0,
    )[0]


def to_experts(rows):
    return lax.all_to_all(rows, "ep", split_axis=0, concat_axis=0, tiled=True)


def outer_sum(left_rows, right_rows):
    return lax.dot_general(
        left_rows, right_rows, (((0,), (0,)), ((), ())), preferred_element_type=f32
    ).astype(bf16)


def row_target(route_rows, place_row, capacity):
    experts = lax.axis_size("ep")
    expert_ids = jnp.arange(experts, dtype=jnp.int32)
    expert_hit = route_rows[:, 0][:, None] == expert_ids[None, :]
    dest_slot = jnp.sum(jnp.where(expert_hit, place_row[None, :], 0), axis=1)
    slot_hit = (dest_slot[:, None] == expert_ids[None, :]).astype(jnp.int32)
    slot_rank = jnp.sum(jnp.cumsum(slot_hit, axis=0) * slot_hit, axis=1) - 1
    return dest_slot * (lax.axis_size("grp") * capacity) + slot_rank


def inverse_of(activation):
    widened = activation.astype(f32)
    return lax.rsqrt(jnp.mean(widened * widened, axis=-1) + 1e-06)


def picker_of(target, row_total):
    return (jnp.arange(row_total, dtype=jnp.int32)[:, None] == target[None, :]).astype(bf16)


def pick(picker, rows):
    return jnp.dot(picker, rows, preferred_element_type=f32).astype(bf16)


def unpick(picker, rows):
    return lax.dot_general(picker, rows, (((0,), (0,)), ((), ())), preferred_element_type=f32)


def below(grad_above, inverse, unit_feat, returned, gain_row):
    width = unit_feat.shape[1]
    d_scaled = returned[:, :width] * gain_row
    mean = (returned[:, width : width + 1] + returned[:, width + 1 : width + 2]) / (
        lax.axis_size("grp") * width
    )
    return (grad_above.astype(f32) + inverse * (d_scaled - unit_feat * mean)).astype(bf16)


def move_ep(array, axis, step):
    cores, side = 2, 4
    pairs = []
    for i in range(lax.axis_size("ep")):
        place = [i // (cores * side), i // cores % side, i % cores]
        place[axis] = (place[axis] + step) % (cores if axis == 2 else side)
        pairs.append((i, (place[0] * side + place[1]) * cores + place[2]))
    return lax.ppermute(array, "ep", pairs)


def sum_side(array, axis):
    opposite = array + move_ep(array, axis, 2)
    return opposite + (move_ep(array, axis, 1) + move_ep(array, axis, 3))


def body(layer_input, middle, upstream, gains, routes, gates, placement, in_proj, out_proj):
    groups = lax.axis_size("grp")
    experts = lax.axis_size("ep")
    here = lax.axis_index("grp")
    tokens = middle.shape[0]
    width = middle.shape[1] // groups
    capacity = 3 * tokens // (2 * experts)
    row_total = groups * experts * capacity
    gain_block = block_of(gains, here, width, 1)

    middle_blocks = feature_blocks(middle)
    middle_slots = send_blocks(middle_blocks)
    middle_t = jnp.stack(middle_slots).reshape(-1, width)
    small = jnp.stack(
        [
            inverse_of(layer_input),
            inverse_of(middle),
            gates[0, :, 0],
            gates[1, :, 0],
            row_target(routes[0], placement[0], capacity).astype(f32),
            row_target(routes[1], placement[1], capacity).astype(f32),
        ]
    )
    small_t = spread_small(after(small, middle_slots[1]))
    inverse = [small_t[:, j].reshape(-1, 1) for j in range(2)]
    gate = [small_t[:, 2 + j].reshape(-1, 1) for j in range(2)]
    ranks = ((here - jnp.arange(groups, dtype=jnp.int32)) % groups * capacity)[:, None]
    picker = [
        picker_of((small_t[:, 4 + j].astype(jnp.int32) + ranks).reshape(-1), row_total)
        for j in range(2)
    ]

    unit_1 = middle_t.astype(f32) * inverse[1]
    features_1 = to_experts(pick(picker[1], (unit_1 * gain_block[1]).astype(bf16)))
    both = feature_blocks(after(jnp.concatenate([upstream, layer_input]), middle_slots[1]))
    both = jnp.stack(send_blocks(both)).reshape(groups, 2, tokens, width)
    upstream_t, input_t = (both[:, part].reshape(-1, width) for part in range(2))
    scaled_1 = (gate[1] * upstream_t.astype(f32)).astype(bf16)
    up_rows_1 = to_experts(pick(picker[1], scaled_1))
    unit_0 = input_t.astype(f32) * inverse[0]

    pre = pre_parts(features_1, in_proj, 1)
    up_rows_1 = to_experts(pick(picker[1], scaled_1))
    pre = scatter_halves(pre)
    back = back_parts(up_rows_1, out_proj, 1)
    features_0 = to_experts(
        pick(after(picker[0], back[0][0]), (unit_0 * gain_block[0]).astype(bf16))
    )
    packed, hidden_1 = quarter_grads(pre, scatter_halves(back))
    pre_0 = pre_parts(after(features_0, packed[0]), in_proj, 0)
    packed = gather_halves(*packed)
    pre_0, packed = lax.optimization_barrier((pre_0, packed))
    d_rows, grads = rows_from_grads(packed, in_proj, 1)
    pre_0 = sum_parts(scatter_halves(pre_0))
    returned = unpick(picker[1], to_experts(d_rows))
    gain_part_1 = jnp.sum(d_rows[:, :width].astype(f32) * features_1.astype(f32), axis=0)
    grad_gate_1 = outer_sum(features_1, grads[0])
    grad_up_1 = outer_sum(features_1, grads[1])

    pre = gather_halves(*pre_0)
    grad_mid = below(upstream_t, inverse[1], unit_1, returned, gain_block[1])
    scaled_0 = (gate[0] * grad_mid.astype(f32)).astype(bf16)
    up_rows_0 = to_experts(pick(picker[0], scaled_0))
    back = back_parts(up_rows_0, out_proj, 0)
    pre, back = lax.optimization_barrier((pre, back))
    hidden_0 = hidden_from_sums(pre)
    back = gather_halves(*sum_parts(scatter_halves(back)))
    grad_down_0 = outer_sum(hidden_0, up_rows_0)
    d_rows, grads = rows_from_sums(pre, back, in_proj, 0)
    returned = to_experts(d_rows)
    hidden_1 = gather_halves(*after(tuple(hidden_1), d_rows))
    gain_part_0 = jnp.sum(d_rows[:, :width].astype(f32) * features_0.astype(f32), axis=0)
    gain_sum = jnp.stack([gain_part_0, gain_part_1]) / gain_block
    gain_sum = gain_sum + move_ep(gain_sum, 2, 1)
    gain_sum = sum_side(gain_sum, 1)
    returned = unpick(after(picker[0], gain_sum), returned)
    grad_low = below(grad_mid, inverse[0], unit_0, returned, gain_block[0])
    grad_input, first_piece = join_features(grad_low)
    hidden_1, gain_sum = lax.optimization_barrier((hidden_1, gain_sum, first_piece))[:2]
    grad_down_1 = outer_sum(join_rows(hidden_1), up_rows_1)
    grad_gate_0 = outer_sum(features_0, grads[0])
    grad_up_0 = outer_sum(features_0, grads[1])
    gain_sum = sum_side(gain_sum, 0)

    grad_gains = jnp.zeros(gains.shape, f32)
    for step in range(groups):
        piece = gain_sum if step == 0 else shift_grp(gain_sum, step)
        grad_gains = lax.dynamic_update_slice(
            grad_gains, piece, (0, (here - step) % groups * width)
        )

    grad_in_proj = jnp.stack(
        [jnp.stack([grad_gate_0, grad_up_0]), jnp.stack([grad_gate_1, grad_up_1])]
    )[:, None]
    grad_out_proj = jnp.stack([grad_down_0, grad_down_1])[:, None]
    return (grad_input, grad_in_proj, grad_out_proj, grad_gains)


def solution(mesh):
    return jax.shard_map(
        body,
        mesh=mesh,
        in_specs=(
            P(("grp", "ep"), None),
            P(("grp", "ep"), None),
            P(("grp", "ep"), None),
            P(),
            P(None, ("grp", "ep"), None),
            P(None, ("grp", "ep"), None),
            P(),
            P(None, "ep", None, "grp", None),
            P(None, "ep", None, "grp"),
        ),
        out_specs=(
            P(("grp", "ep"), None),
            P(None, "ep", None, "grp", None),
            P(None, "ep", None, "grp"),
            P(),
        ),
        check_vma=False,
    )
```

```python
import jax
import jax.numpy as jnp
from jax import lax
from jax.experimental import pallas as pl
from jax.experimental.pallas import tpu as pltpu
from jax.sharding import PartitionSpec as P

f32 = jnp.float32
bf16 = jnp.bfloat16
LANES = 128
DOTS = 112


def shift_grp(array, step):
    groups = lax.axis_size("grp")
    pairs = [(i, (i + step) % groups) for i in range(groups)]
    return lax.ppermute(array, "grp", pairs)


def block_of(array, index, extent, axis):
    return lax.dynamic_slice_in_dim(array, index * extent, extent, axis)


def feature_blocks(array):
    groups = lax.axis_size("grp")
    here = lax.axis_index("grp")
    width = array.shape[1] // groups
    return [block_of(array, (here + step) % groups, width, 1) for step in range(groups)]


def send_blocks(blocks):
    return [block if step == 0 else shift_grp(block, step) for step, block in enumerate(blocks)]


def join_features(rows):
    groups = lax.axis_size("grp")
    here = lax.axis_index("grp")
    width = rows.shape[1]
    slots = rows.reshape(groups, -1, width)
    pieces = [slots[0]] + [shift_grp(slots[step], -step) for step in range(1, groups)]
    whole = jnp.zeros((slots.shape[1], groups * width), rows.dtype)
    for step, piece in enumerate(pieces):
        whole = lax.dynamic_update_slice(whole, piece, (0, (here + step) % groups * width))
    return whole, pieces[1]


def spread_small(array):
    groups = lax.axis_size("grp")
    return jnp.stack([array] + [shift_grp(array, step) for step in range(1, groups)])


def after(array, *others):
    return lax.optimization_barrier((array,) + others)[0]


def send_chunks(chunks):
    return [chunk if step == 0 else shift_grp(chunk, step) for step, chunk in enumerate(chunks)]


def scatter_halves(halves):
    own, right, far, left = halves
    from_left, from_right = shift_grp(far[0], 1), shift_grp(far[1], -1)
    left_bottom, right_top = shift_grp(right[1], 1), shift_grp(left[0], -1)
    left_top = shift_grp((right[0].astype(f32) + from_left.astype(f32)).astype(bf16), 1)
    right_sum = (left[1].astype(f32) + from_right.astype(f32)).astype(bf16)
    right_bottom = shift_grp(right_sum, -1)
    return ((own[0], left_top, right_top), (own[1], left_bottom, right_bottom)), right_sum


def gather_halves(top, bottom):
    left, right = (shift_grp(top, 1), shift_grp(bottom, 1)), (shift_grp(top, -1), shift_grp(bottom, -1))
    far = shift_grp(left[0], 1), shift_grp(right[1], -1)
    return (top, bottom), right, far, left


def flat(pairs):
    return [half for pair in pairs for half in pair]


def call(kernel, grid_args, out_shapes, flops, scratch=()):
    in_specs = []
    for array, block, index in grid_args:
        shape = array.shape if block is None else block
        place = (0,) * len(shape) if index is None else index
        in_specs.append(pl.BlockSpec(shape, lambda i, here, place=place: place))
    out_specs = [
        pl.BlockSpec(shape.shape, lambda i, here, n=len(shape.shape): (0,) * n)
        for shape in out_shapes
    ]
    moved = sum(array.size * array.dtype.itemsize for array, block, _ in grid_args if block is None)
    moved += sum(shape.size * shape.dtype.itemsize for shape in out_shapes)
    return pl.pallas_call(
        kernel,
        grid_spec=pltpu.PrefetchScalarGridSpec(
            num_scalar_prefetch=1, grid=(1,), in_specs=in_specs, out_specs=out_specs,
            scratch_shapes=scratch,
        ),
        out_shape=out_shapes,
        compiler_params=pltpu.CompilerParams(vmem_limit_bytes=48 * 1024 * 1024),
        cost_estimate=pl.CostEstimate(flops=flops, bytes_accessed=moved, transcendentals=0),
    )(lax.axis_index("grp").reshape(1), *(array for array, _, _ in grid_args))


def nn(left, right):
    return lax.dot_general(left, right, (((1,), (0,)), ((), ())), preferred_element_type=f32)


def nt(left, right):
    return lax.dot_general(left, right, (((1,), (1,)), ((), ())), preferred_element_type=f32)


def rows_at(here, step, rows):
    groups = 4
    return pl.ds(pl.multiple_of((here + step) % groups * rows, 16), rows)


def turn(here, turned, x_ref, rows):
    for step in range(4):
        turned[step * rows : (step + 1) * rows, :] = x_ref[rows_at(here[0], step, rows), :]


def pre_parts(features, in_proj, layer, pieces):
    rows, units = features.shape[0] // 4, in_proj.shape[-1]
    size = rows // pieces

    def kernel(here, x_ref, w_ref, *refs):
        outs, turned = refs[:-1], refs[-1]
        turn(here, turned, x_ref, rows)
        for part in range(2):
            whole = nn(turned[...], w_ref[0, 0, part]).astype(bf16)
            for place, out in enumerate(outs):
                out[part] = whole[place * size : (place + 1) * size]

    outs = call(
        kernel,
        [(features, None, None), (in_proj, (1, 1) + in_proj.shape[2:], (layer, 0, 0, 0, 0))],
        [jax.ShapeDtypeStruct((2, size, units), bf16)] * (4 * pieces),
        4 * features.size * units,
        [pltpu.VMEM(features.shape, bf16)],
    )
    return [outs[pieces * step : pieces * (step + 1)] for step in range(4)]


def back_parts(up_rows, out_proj, layer):
    rows, units = up_rows.shape[0] // 4, out_proj.shape[2]
    half = rows // 2

    def kernel(here, x_ref, w_ref, *refs):
        outs, turned = refs[:8], refs[8]
        turn(here, turned, x_ref, rows)
        whole = nt(turned[...], w_ref[0, 0]).astype(bf16)
        for place in range(8):
            outs[place][...] = whole[place * half : (place + 1) * half]

    outs = call(
        kernel,
        [(up_rows, None, None), (out_proj, (1, 1) + out_proj.shape[2:], (layer, 0, 0, 0))],
        [jax.ShapeDtypeStruct((half, units), bf16)] * 8,
        2 * up_rows.size * units,
        [pltpu.VMEM(up_rows.shape, bf16)],
    )
    return [outs[2 * step : 2 * step + 2] for step in range(4)]


def grads_of(pre_gate, pre_up, back_hidden):
    sigmoid_gate = jax.nn.sigmoid(pre_gate)
    active = pre_gate * sigmoid_gate
    d_gate = back_hidden * pre_up * sigmoid_gate * (1.0 + pre_gate * (1.0 - sigmoid_gate))
    d_gate, d_up = d_gate.astype(bf16), (back_hidden * active).astype(bf16)
    dots = d_gate.astype(f32) * pre_gate + d_up.astype(f32) * pre_up
    dots = jnp.sum(dots, axis=-1, keepdims=True)
    high = dots.astype(bf16).astype(f32)
    lane = lax.broadcasted_iota(jnp.int32, (dots.shape[0], LANES), 1)
    tail = jnp.where(lane == DOTS, high, jnp.where(lane == DOTS + 1, dots - high, 0.0)).astype(bf16)
    return (active * pre_up).astype(bf16), d_gate, d_up, tail


def total(refs, *index):
    value = refs[0][index].astype(f32)
    for ref in refs[1:]:
        value = value + ref[index].astype(f32)
    return value


def quarter_grads(pres, backs):
    half, units = backs[0][0].shape

    def kernel(here, *refs):
        for side in range(2):
            pre, back = refs[3 * side : 3 * side + 3], refs[6 + 3 * side : 9 + 3 * side]
            packed, hidden_ref = refs[12 + side], refs[14 + side]
            hidden, d_gate, d_up, tail = grads_of(total(pre, 0), total(pre, 1), total(back, ...))
            packed[:, :units] = d_gate
            packed[:, units : 2 * units] = d_up
            packed[:, 2 * units :] = tail
            hidden_ref[...] = hidden

    packed = jax.ShapeDtypeStruct((half, 2 * units + LANES), bf16)
    hidden = jax.ShapeDtypeStruct((half, units), bf16)
    outs = call(
        kernel,
        [(array, None, None) for array in flat(pres) + flat(backs)],
        [packed, packed, hidden, hidden],
        0,
    )
    return outs[:2], outs[2:]


def sum_parts(parts):
    def kernel(here, *refs):
        for side in range(2):
            refs[6 + side][...] = total(refs[3 * side : 3 * side + 3], ...).astype(bf16)

    return call(
        kernel,
        [(part, None, None) for part in flat(parts)],
        [jax.ShapeDtypeStruct(parts[0][0].shape, bf16)] * 2,
        0,
    )


def sum_whole(parts):
    layers, rows, units = parts[0].shape
    half = rows // 2

    def kernel(here, *refs):
        for side in range(2):
            at = slice(side * half, (side + 1) * half)
            refs[4 + side][...] = total(refs[:4], slice(None), at, slice(None)).astype(bf16)

    return call(
        kernel,
        [(part, None, None) for part in parts],
        [jax.ShapeDtypeStruct((layers, half, units), bf16)] * 2,
        0,
    )


def places(here, half):
    return [
        pl.ds(pl.multiple_of((here[0] + k // 2) % 4 * (2 * half) + k % 2 * half, 16), half)
        for k in range(8)
    ]


def store_rows(out, width, grads, w_ref, features):
    d_rows = (nt(grads[0], w_ref[0, 0, 0]) + nt(grads[1], w_ref[0, 0, 1])).astype(bf16)
    out[:, :width] = d_rows
    gain = jnp.sum(d_rows.astype(f32) * features[...].astype(f32), axis=0, keepdims=True)
    row = lax.broadcasted_iota(jnp.int32, (8, LANES), 0)
    lane = lax.broadcasted_iota(jnp.int32, (8, LANES), 1)
    rest = LANES - DOTS
    value = jnp.zeros((8, LANES), f32)
    for tile in range(width // LANES):
        same = jnp.broadcast_to(gain[:, tile * LANES : (tile + 1) * LANES], (8, LANES))
        last = pltpu.roll(same, (rest * tile - DOTS) % LANES, 1)
        in_last = (row == 7) & (lane >= rest * tile) & (lane < rest * (tile + 1))
        value = value + jnp.where(row == tile, same, jnp.where(in_last, last, 0.0))
    high = value.astype(bf16).astype(f32)
    middle = (value - high).astype(bf16).astype(f32)
    parts = jnp.concatenate([high, middle, value - high - middle], axis=0)
    buckets = out.shape[0] // 24
    parts = jnp.broadcast_to(parts[None], (buckets, 24, LANES)).reshape(out.shape[0], LANES)
    lane = lax.broadcasted_iota(jnp.int32, parts.shape, 1)
    tail = jnp.where(lane < DOTS, parts, out[:, width:].astype(f32))
    out[:, width:] = tail.astype(bf16)


def gain_of(raw, width):
    tiles = width // LANES
    total = raw[:, width : width + DOTS].astype(f32).reshape(-1, 3, 8, DOTS)
    total = jnp.sum(total, axis=(0, 1))
    last = total[7].reshape(7, LANES - DOTS)[:tiles]
    return jnp.concatenate([total[:tiles], last], axis=1).reshape(width)


def rows_from_grads(pieces, in_proj, layer, features):
    half, width, units = pieces[0][0].shape[0], in_proj.shape[3], in_proj.shape[4]

    def kernel(here, *refs):
        w_ref, features, out, grads = refs[8:]
        for piece, at in zip(refs[:8], places(here, half)):
            grads[0, at, :] = piece[:, :units]
            grads[1, at, :] = piece[:, units : 2 * units]
            out[at, width:] = piece[:, 2 * units :]
        store_rows(out, width, grads, w_ref, features)

    return call(
        kernel,
        [(piece, None, None) for piece in flat(pieces)]
        + [(in_proj, (1, 1) + in_proj.shape[2:], (layer, 0, 0, 0, 0)), (features, None, None)],
        [
            jax.ShapeDtypeStruct((8 * half, width + LANES), bf16),
            jax.ShapeDtypeStruct((2, 8 * half, units), bf16),
        ],
        32 * half * width * units,
    )


def rows_from_sums(pres, backs, in_proj, layer, features):
    (half, units), width = backs[0][0].shape, in_proj.shape[3]

    def kernel(here, *refs):
        pre, back, (w_ref, features, out, grads) = refs[:8], refs[8:16], refs[16:]
        for k, at in enumerate(places(here, half)):
            _, d_gate, d_up, tail = grads_of(
                pre[k][0].astype(f32), pre[k][1].astype(f32), back[k][...].astype(f32)
            )
            grads[0, at, :] = d_gate
            grads[1, at, :] = d_up
            out[at, width:] = tail
        store_rows(out, width, grads, w_ref, features)

    return call(
        kernel,
        [(array, None, None) for array in flat(pres) + flat(backs)]
        + [(in_proj, (1, 1) + in_proj.shape[2:], (layer, 0, 0, 0, 0)), (features, None, None)],
        [
            jax.ShapeDtypeStruct((8 * half, width + LANES), bf16),
            jax.ShapeDtypeStruct((2, 8 * half, units), bf16),
        ],
        32 * half * width * units,
    )


def hidden_from_sums(pres):
    _, half, units = pres[0][0].shape

    def kernel(here, *refs):
        for pre, at in zip(refs[:8], places(here, half)):
            gate = pre[0].astype(f32)
            hidden = gate * jax.nn.sigmoid(gate) * pre[1].astype(f32)
            refs[8][at, :] = hidden.astype(bf16)

    return call(
        kernel,
        [(pre, None, None) for pre in flat(pres)],
        [jax.ShapeDtypeStruct((8 * half, units), bf16)],
        0,
    )[0]


def join_rows(pieces):
    half, units = pieces[0][0].shape

    def kernel(here, *refs):
        for piece, at in zip(refs[:8], places(here, half)):
            refs[8][at, :] = piece[...]

    return call(
        kernel,
        [(piece, None, None) for piece in flat(pieces)],
        [jax.ShapeDtypeStruct((8 * half, units), bf16)],
        0,
    )[0]


def to_experts(rows):
    return lax.all_to_all(rows, "ep", split_axis=0, concat_axis=0, tiled=True)


def outer_into(buffer, layer, left, right, tiles):
    rows, high = left.shape
    wide = right.shape[-1]
    if right.ndim == 3:
        shape, block = (2, 1, tiles, high, wide), (1, 1, 1, high, wide)
        left_spec = pl.BlockSpec((rows, high), lambda i: (0, 0))
        right_spec = pl.BlockSpec((1, rows, wide), lambda i: (i, 0, 0))
        out_spec = pl.BlockSpec(block, lambda i: (layer, 0, i, 0, 0))
    else:
        shape, block = (2, 1, high, wide), (1, 1, high // tiles, wide)
        left_spec = pl.BlockSpec((rows, high // tiles), lambda i: (0, i))
        right_spec = pl.BlockSpec((rows, wide), lambda i: (0, 0))
        out_spec = pl.BlockSpec(block, lambda i: (layer, 0, i, 0))

    def kernel(left_ref, right_ref, *refs):
        out = refs[-1]
        value = right_ref[...].reshape(rows, wide)
        total = lax.dot_general(
            left_ref[...], value, (((0,), (0,)), ((), ())), preferred_element_type=f32
        )
        out[...] = total.astype(bf16).reshape(out.shape)

    arrays, specs, aliases = [left, right], [left_spec, right_spec], {}
    if buffer is not None:
        arrays, specs, aliases = arrays + [buffer], specs + [pl.BlockSpec(memory_space=pl.ANY)], {2: 0}
    return pl.pallas_call(
        kernel,
        grid=(tiles,),
        in_specs=specs,
        out_specs=out_spec,
        out_shape=jax.ShapeDtypeStruct(shape, bf16),
        input_output_aliases=aliases,
        compiler_params=pltpu.CompilerParams(vmem_limit_bytes=48 * 1024 * 1024),
        cost_estimate=pl.CostEstimate(
            flops=2 * right.size * high,
            bytes_accessed=2 * (left.size + right.size) + 2 * tiles * high * wide,
            transcendentals=0,
        ),
    )(*arrays)


def row_target(route_rows, place_row, capacity):
    experts = lax.axis_size("ep")
    expert_ids = jnp.arange(experts, dtype=jnp.int32)
    expert_hit = route_rows[:, 0][:, None] == expert_ids[None, :]
    dest_slot = jnp.sum(jnp.where(expert_hit, place_row[None, :], 0), axis=1)
    slot_hit = (dest_slot[:, None] == expert_ids[None, :]).astype(jnp.int32)
    slot_rank = jnp.sum(jnp.cumsum(slot_hit, axis=0) * slot_hit, axis=1) - 1
    return dest_slot * (lax.axis_size("grp") * capacity) + slot_rank


def inverse_of(activation):
    widened = activation.astype(f32)
    return lax.rsqrt(jnp.mean(widened * widened, axis=-1) + 1e-06)


def picker_of(target, row_total):
    return (jnp.arange(row_total, dtype=jnp.int32)[:, None] == target[None, :]).astype(bf16)


def pick(picker, rows):
    return jnp.dot(picker, rows, preferred_element_type=f32).astype(bf16)


def unpick(picker, rows):
    return lax.dot_general(picker, rows, (((0,), (0,)), ((), ())), preferred_element_type=f32)


def below(grad_above, inverse, unit_feat, returned, gain_row):
    width = unit_feat.shape[1]
    d_scaled = returned[:, :width] * gain_row
    first = width + DOTS
    mean = (returned[:, first : first + 1] + returned[:, first + 1 : first + 2]) / (
        lax.axis_size("grp") * width
    )
    return (grad_above.astype(f32) + inverse * (d_scaled - unit_feat * mean)).astype(bf16)


def body(layer_input, middle, upstream, gains, routes, gates, placement, in_proj, out_proj):
    groups = lax.axis_size("grp")
    experts = lax.axis_size("ep")
    here = lax.axis_index("grp")
    tokens = middle.shape[0]
    width = middle.shape[1] // groups
    capacity = 3 * tokens // (2 * experts)
    row_total = groups * experts * capacity
    gain_block = block_of(gains, here, width, 1)

    middle_blocks = feature_blocks(middle)
    middle_slots = send_blocks(middle_blocks)
    middle_t = jnp.stack(middle_slots).reshape(-1, width)
    small = jnp.stack(
        [
            inverse_of(layer_input),
            inverse_of(middle),
            gates[0, :, 0],
            gates[1, :, 0],
            row_target(routes[0], placement[0], capacity).astype(f32),
            row_target(routes[1], placement[1], capacity).astype(f32),
        ]
    )
    small_t = spread_small(after(small, middle_slots[1]))
    inverse = [small_t[:, j].reshape(-1, 1) for j in range(2)]
    gate = [small_t[:, 2 + j].reshape(-1, 1) for j in range(2)]
    ranks = ((here - jnp.arange(groups, dtype=jnp.int32)) % groups * capacity)[:, None]
    picker = [
        picker_of((small_t[:, 4 + j].astype(jnp.int32) + ranks).reshape(-1), row_total)
        for j in range(2)
    ]

    unit_1 = middle_t.astype(f32) * inverse[1]
    features_1 = to_experts(pick(picker[1], (unit_1 * gain_block[1]).astype(bf16)))
    both = feature_blocks(after(jnp.concatenate([upstream, layer_input]), middle_slots[1]))
    both = jnp.stack(send_blocks(both)).reshape(groups, 2, tokens, width)
    upstream_t, input_t = (both[:, part].reshape(-1, width) for part in range(2))
    scaled_1 = (gate[1] * upstream_t.astype(f32)).astype(bf16)
    up_rows_1 = to_experts(pick(picker[1], scaled_1))
    unit_0 = input_t.astype(f32) * inverse[0]

    pre = pre_parts(features_1, in_proj, 1, 2)
    up_rows_1 = to_experts(pick(picker[1], scaled_1))
    pre, _ = scatter_halves(pre)
    back = back_parts(up_rows_1, out_proj, 1)
    features_0 = to_experts(
        pick(after(picker[0], back[0][0]), (unit_0 * gain_block[0]).astype(bf16))
    )
    back, _ = scatter_halves(back)
    packed, hidden_1 = quarter_grads(pre, back)
    pre_0 = flat(pre_parts(after(features_0, packed[0]), in_proj, 0, 1))
    packed = gather_halves(*packed)
    pre_0, packed = lax.optimization_barrier((pre_0, packed))
    d_rows, grads_1 = rows_from_grads(packed, in_proj, 1, features_1)
    pre_0 = sum_whole(send_chunks(pre_0))
    raw_1 = to_experts(d_rows)
    returned = unpick(picker[1], raw_1)

    pre = gather_halves(*pre_0)
    grad_mid = below(upstream_t, inverse[1], unit_1, returned, gain_block[1])
    scaled_0 = (gate[0] * grad_mid.astype(f32)).astype(bf16)
    up_rows_0 = to_experts(pick(picker[0], scaled_0))
    back = back_parts(up_rows_0, out_proj, 0)
    grads_1 = after(grads_1, back[0][0])
    grad_in_proj = outer_into(None, 1, features_1, grads_1, 2)
    pre, back = lax.optimization_barrier((pre, back))
    hidden_0 = hidden_from_sums(pre)
    grad_out_proj = outer_into(None, 0, hidden_0, up_rows_0, 2)
    back = gather_halves(*sum_parts(scatter_halves(back)[0]))
    back, grad_in_proj, grad_out_proj = lax.optimization_barrier(
        (back, grad_in_proj, grad_out_proj)
    )
    d_rows, grads = rows_from_sums(pre, back, in_proj, 0, features_0)
    raw_0 = to_experts(d_rows)
    hidden_1 = join_rows(gather_halves(*after(tuple(hidden_1), d_rows)))
    grad_in_proj = outer_into(grad_in_proj, 0, features_0, grads, 2)
    picker_0, grad_in_proj, hidden_1 = lax.optimization_barrier(
        (picker[0], grad_in_proj, hidden_1)
    )
    returned = unpick(picker_0, raw_0)
    grad_low = below(grad_mid, inverse[0], unit_0, returned, gain_block[0])
    grad_input, first_piece = join_features(grad_low)
    hidden_1, raw_0 = lax.optimization_barrier((hidden_1, raw_0, first_piece))[:2]
    grad_out_proj = outer_into(grad_out_proj, 1, hidden_1, up_rows_1, 2)
    gain_sum = jnp.stack([gain_of(raw_0, width), gain_of(raw_1, width)]) / gain_block

    grad_gains = jnp.zeros(gains.shape, f32)
    for step in range(groups):
        piece = gain_sum if step == 0 else shift_grp(gain_sum, step)
        grad_gains = lax.dynamic_update_slice(
            grad_gains, piece, (0, (here - step) % groups * width)
        )

    return (grad_input, grad_in_proj, grad_out_proj, grad_gains)


def solution(mesh):
    return jax.shard_map(
        body,
        mesh=mesh,
        in_specs=(
            P(("grp", "ep"), None),
            P(("grp", "ep"), None),
            P(("grp", "ep"), None),
            P(),
            P(None, ("grp", "ep"), None),
            P(None, ("grp", "ep"), None),
            P(),
            P(None, "ep", None, "grp", None),
            P(None, "ep", None, "grp"),
        ),
        out_specs=(
            P(("grp", "ep"), None),
            P(None, "ep", None, "grp", None),
            P(None, "ep", None, "grp"),
            P(),
        ),
        check_vma=False,
    )
```

```python
import jax
import jax.numpy as jnp
from jax import lax
from jax.experimental import pallas as pl
from jax.experimental.pallas import tpu as pltpu
from jax.sharding import PartitionSpec as P

f32 = jnp.float32
bf16 = jnp.bfloat16
LANES = 128
DOTS = 112


def shift_grp(array, step):
    groups = lax.axis_size("grp")
    pairs = [(i, (i + step) % groups) for i in range(groups)]
    return lax.ppermute(array, "grp", pairs)


def block_of(array, index, extent, axis):
    return lax.dynamic_slice_in_dim(array, index * extent, extent, axis)


def feature_blocks(array):
    groups = lax.axis_size("grp")
    here = lax.axis_index("grp")
    width = array.shape[1] // groups
    return [block_of(array, (here + step) % groups, width, 1) for step in range(groups)]


def send_blocks(blocks):
    return [block if step == 0 else shift_grp(block, step) for step, block in enumerate(blocks)]


def join_features(rows):
    groups = lax.axis_size("grp")
    here = lax.axis_index("grp")
    width = rows.shape[1]
    slots = rows.reshape(groups, -1, width)
    pieces = [slots[0]] + [shift_grp(slots[step], -step) for step in range(1, groups)]
    whole = jnp.zeros((slots.shape[1], groups * width), rows.dtype)
    for step, piece in enumerate(pieces):
        whole = lax.dynamic_update_slice(whole, piece, (0, (here + step) % groups * width))
    return whole, pieces[1]


def spread_small(array):
    groups = lax.axis_size("grp")
    return jnp.stack([array] + [shift_grp(array, step) for step in range(1, groups)])


def after(array, *others):
    return lax.optimization_barrier((array,) + others)[0]


def send_chunks(chunks):
    return [chunk if step == 0 else shift_grp(chunk, step) for step, chunk in enumerate(chunks)]


def scatter_halves(halves):
    own, right, far, left = halves
    from_left, from_right = shift_grp(far[0], 1), shift_grp(far[1], -1)
    left_bottom, right_top = shift_grp(right[1], 1), shift_grp(left[0], -1)
    left_top = shift_grp((right[0].astype(f32) + from_left.astype(f32)).astype(bf16), 1)
    right_sum = (left[1].astype(f32) + from_right.astype(f32)).astype(bf16)
    right_bottom = shift_grp(right_sum, -1)
    return ((own[0], left_top, right_top), (own[1], left_bottom, right_bottom)), right_sum


def gather_halves(top, bottom):
    left, right = (shift_grp(top, 1), shift_grp(bottom, 1)), (shift_grp(top, -1), shift_grp(bottom, -1))
    far = shift_grp(left[0], 1), shift_grp(right[1], -1)
    return (top, bottom), right, far, left


def flat(pairs):
    return [half for pair in pairs for half in pair]


def call(kernel, grid_args, out_shapes, flops, scratch=()):
    in_specs = []
    for array, block, index in grid_args:
        shape = array.shape if block is None else block
        place = (0,) * len(shape) if index is None else index
        in_specs.append(pl.BlockSpec(shape, lambda i, here, place=place: place))
    out_specs = [
        pl.BlockSpec(shape.shape, lambda i, here, n=len(shape.shape): (0,) * n)
        for shape in out_shapes
    ]
    moved = sum(array.size * array.dtype.itemsize for array, block, _ in grid_args if block is None)
    moved += sum(shape.size * shape.dtype.itemsize for shape in out_shapes)
    return pl.pallas_call(
        kernel,
        grid_spec=pltpu.PrefetchScalarGridSpec(
            num_scalar_prefetch=1, grid=(1,), in_specs=in_specs, out_specs=out_specs,
            scratch_shapes=scratch,
        ),
        out_shape=out_shapes,
        compiler_params=pltpu.CompilerParams(vmem_limit_bytes=48 * 1024 * 1024),
        cost_estimate=pl.CostEstimate(flops=flops, bytes_accessed=moved, transcendentals=0),
    )(lax.axis_index("grp").reshape(1), *(array for array, _, _ in grid_args))


def nn(left, right):
    return lax.dot_general(left, right, (((1,), (0,)), ((), ())), preferred_element_type=f32)


def nt(left, right):
    return lax.dot_general(left, right, (((1,), (1,)), ((), ())), preferred_element_type=f32)


def rows_at(here, step, rows):
    groups = 4
    return pl.ds(pl.multiple_of((here + step) % groups * rows, 16), rows)


def turn(here, turned, x_ref, rows):
    for step in range(4):
        turned[step * rows : (step + 1) * rows, :] = x_ref[rows_at(here[0], step, rows), :]


def pre_parts(features, in_proj, layer, pieces):
    rows, units = features.shape[0] // 4, in_proj.shape[-1]
    size = rows // pieces

    def kernel(here, x_ref, w_ref, *refs):
        outs, turned = refs[:-1], refs[-1]
        turn(here, turned, x_ref, rows)
        for part in range(2):
            whole = nn(turned[...], w_ref[0, 0, part]).astype(bf16)
            for place, out in enumerate(outs):
                out[part] = whole[place * size : (place + 1) * size]

    outs = call(
        kernel,
        [(features, None, None), (in_proj, (1, 1) + in_proj.shape[2:], (layer, 0, 0, 0, 0))],
        [jax.ShapeDtypeStruct((2, size, units), bf16)] * (4 * pieces),
        4 * features.size * units,
        [pltpu.VMEM(features.shape, bf16)],
    )
    return [outs[pieces * step : pieces * (step + 1)] for step in range(4)]


def back_parts(up_rows, out_proj, layer):
    rows, units = up_rows.shape[0] // 4, out_proj.shape[2]
    half = rows // 2

    def kernel(here, x_ref, w_ref, *refs):
        outs, turned = refs[:8], refs[8]
        turn(here, turned, x_ref, rows)
        whole = nt(turned[...], w_ref[0, 0]).astype(bf16)
        for place in range(8):
            outs[place][...] = whole[place * half : (place + 1) * half]

    outs = call(
        kernel,
        [(up_rows, None, None), (out_proj, (1, 1) + out_proj.shape[2:], (layer, 0, 0, 0))],
        [jax.ShapeDtypeStruct((half, units), bf16)] * 8,
        2 * up_rows.size * units,
        [pltpu.VMEM(up_rows.shape, bf16)],
    )
    return [outs[2 * step : 2 * step + 2] for step in range(4)]


def grads_of(pre_gate, pre_up, back_hidden):
    sigmoid_gate = jax.nn.sigmoid(pre_gate)
    active = pre_gate * sigmoid_gate
    d_gate = back_hidden * pre_up * sigmoid_gate * (1.0 + pre_gate * (1.0 - sigmoid_gate))
    d_gate, d_up = d_gate.astype(bf16), (back_hidden * active).astype(bf16)
    dots = d_gate.astype(f32) * pre_gate + d_up.astype(f32) * pre_up
    dots = jnp.sum(dots, axis=-1, keepdims=True)
    high = dots.astype(bf16).astype(f32)
    lane = lax.broadcasted_iota(jnp.int32, (dots.shape[0], LANES), 1)
    tail = jnp.where(lane == DOTS, high, jnp.where(lane == DOTS + 1, dots - high, 0.0)).astype(bf16)
    return (active * pre_up).astype(bf16), d_gate, d_up, tail


def total(refs, *index):
    value = refs[0][index].astype(f32)
    for ref in refs[1:]:
        value = value + ref[index].astype(f32)
    return value


def quarter_grads(pres, backs):
    half, units = backs[0][0].shape

    def kernel(here, *refs):
        for side in range(2):
            pre, back = refs[3 * side : 3 * side + 3], refs[6 + 3 * side : 9 + 3 * side]
            packed, hidden_ref = refs[12 + side], refs[14 + side]
            hidden, d_gate, d_up, tail = grads_of(total(pre, 0), total(pre, 1), total(back, ...))
            packed[:, :units] = d_gate
            packed[:, units : 2 * units] = d_up
            packed[:, 2 * units :] = tail
            hidden_ref[...] = hidden

    packed = jax.ShapeDtypeStruct((half, 2 * units + LANES), bf16)
    hidden = jax.ShapeDtypeStruct((half, units), bf16)
    outs = call(
        kernel,
        [(array, None, None) for array in flat(pres) + flat(backs)],
        [packed, packed, hidden, hidden],
        0,
    )
    return outs[:2], outs[2:]


def sum_parts(parts):
    def kernel(here, *refs):
        for side in range(2):
            refs[6 + side][...] = total(refs[3 * side : 3 * side + 3], ...).astype(bf16)

    return call(
        kernel,
        [(part, None, None) for part in flat(parts)],
        [jax.ShapeDtypeStruct(parts[0][0].shape, bf16)] * 2,
        0,
    )


def sum_whole(parts):
    layers, rows, units = parts[0].shape
    half = rows // 2

    def kernel(here, *refs):
        for side in range(2):
            at = slice(side * half, (side + 1) * half)
            refs[4 + side][...] = total(refs[:4], slice(None), at, slice(None)).astype(bf16)

    return call(
        kernel,
        [(part, None, None) for part in parts],
        [jax.ShapeDtypeStruct((layers, half, units), bf16)] * 2,
        0,
    )


def places(here, half):
    return [
        pl.ds(pl.multiple_of((here[0] + k // 2) % 4 * (2 * half) + k % 2 * half, 16), half)
        for k in range(8)
    ]


def store_rows(out, width, grads, w_ref, features):
    d_rows = (nt(grads[0], w_ref[0, 0, 0]) + nt(grads[1], w_ref[0, 0, 1])).astype(bf16)
    out[:, :width] = d_rows
    gain = jnp.sum(d_rows.astype(f32) * features[...].astype(f32), axis=0, keepdims=True)
    row = lax.broadcasted_iota(jnp.int32, (8, LANES), 0)
    lane = lax.broadcasted_iota(jnp.int32, (8, LANES), 1)
    rest = LANES - DOTS
    value = jnp.zeros((8, LANES), f32)
    for tile in range(width // LANES):
        same = jnp.broadcast_to(gain[:, tile * LANES : (tile + 1) * LANES], (8, LANES))
        last = pltpu.roll(same, (rest * tile - DOTS) % LANES, 1)
        in_last = (row == 7) & (lane >= rest * tile) & (lane < rest * (tile + 1))
        value = value + jnp.where(row == tile, same, jnp.where(in_last, last, 0.0))
    high = value.astype(bf16).astype(f32)
    middle = (value - high).astype(bf16).astype(f32)
    parts = jnp.concatenate([high, middle, value - high - middle], axis=0)
    buckets = out.shape[0] // 24
    parts = jnp.broadcast_to(parts[None], (buckets, 24, LANES)).reshape(out.shape[0], LANES)
    lane = lax.broadcasted_iota(jnp.int32, parts.shape, 1)
    tail = jnp.where(lane < DOTS, parts, out[:, width:].astype(f32))
    out[:, width:] = tail.astype(bf16)


def gain_of(raw, width):
    tiles = width // LANES
    total = raw[:, width : width + DOTS].astype(f32).reshape(-1, 3, 8, DOTS)
    total = jnp.sum(total, axis=(0, 1))
    last = total[7].reshape(7, LANES - DOTS)[:tiles]
    return jnp.concatenate([total[:tiles], last], axis=1).reshape(width)


def rows_from_grads(pieces, in_proj, layer, features):
    half, width, units = pieces[0][0].shape[0], in_proj.shape[3], in_proj.shape[4]

    def kernel(here, *refs):
        w_ref, features, out, grads = refs[8:]
        for piece, at in zip(refs[:8], places(here, half)):
            grads[0, at, :] = piece[:, :units]
            grads[1, at, :] = piece[:, units : 2 * units]
            out[at, width:] = piece[:, 2 * units :]
        store_rows(out, width, grads, w_ref, features)

    return call(
        kernel,
        [(piece, None, None) for piece in flat(pieces)]
        + [(in_proj, (1, 1) + in_proj.shape[2:], (layer, 0, 0, 0, 0)), (features, None, None)],
        [
            jax.ShapeDtypeStruct((8 * half, width + LANES), bf16),
            jax.ShapeDtypeStruct((2, 8 * half, units), bf16),
        ],
        32 * half * width * units,
    )


def rows_from_sums(pres, backs, in_proj, layer, features):
    (half, units), width = backs[0][0].shape, in_proj.shape[3]

    def kernel(here, *refs):
        pre, back, (w_ref, features, out, grads) = refs[:8], refs[8:16], refs[16:]
        for k, at in enumerate(places(here, half)):
            _, d_gate, d_up, tail = grads_of(
                pre[k][0].astype(f32), pre[k][1].astype(f32), back[k][...].astype(f32)
            )
            grads[0, at, :] = d_gate
            grads[1, at, :] = d_up
            out[at, width:] = tail
        store_rows(out, width, grads, w_ref, features)

    return call(
        kernel,
        [(array, None, None) for array in flat(pres) + flat(backs)]
        + [(in_proj, (1, 1) + in_proj.shape[2:], (layer, 0, 0, 0, 0)), (features, None, None)],
        [
            jax.ShapeDtypeStruct((8 * half, width + LANES), bf16),
            jax.ShapeDtypeStruct((2, 8 * half, units), bf16),
        ],
        32 * half * width * units,
    )


def hidden_from_sums(pres):
    _, half, units = pres[0][0].shape

    def kernel(here, *refs):
        for pre, at in zip(refs[:8], places(here, half)):
            gate = pre[0].astype(f32)
            hidden = gate * jax.nn.sigmoid(gate) * pre[1].astype(f32)
            refs[8][at, :] = hidden.astype(bf16)

    return call(
        kernel,
        [(pre, None, None) for pre in flat(pres)],
        [jax.ShapeDtypeStruct((8 * half, units), bf16)],
        0,
    )[0]


def join_rows(pieces):
    half, units = pieces[0][0].shape

    def kernel(here, *refs):
        for piece, at in zip(refs[:8], places(here, half)):
            refs[8][at, :] = piece[...]

    return call(
        kernel,
        [(piece, None, None) for piece in flat(pieces)],
        [jax.ShapeDtypeStruct((8 * half, units), bf16)],
        0,
    )[0]


def to_experts(rows):
    return lax.all_to_all(rows, "ep", split_axis=0, concat_axis=0, tiled=True)


def outer_into(buffer, layer, left, right, tiles):
    rows, high = left.shape
    wide = right.shape[-1]
    if right.ndim == 3:
        shape, block = (2, 1, tiles, high, wide), (1, 1, 1, high, wide)
        left_spec = pl.BlockSpec((rows, high), lambda i: (0, 0))
        right_spec = pl.BlockSpec((1, rows, wide), lambda i: (i, 0, 0))
        out_spec = pl.BlockSpec(block, lambda i: (layer, 0, i, 0, 0))
    else:
        shape, block = (2, 1, high, wide), (1, 1, high // tiles, wide)
        left_spec = pl.BlockSpec((rows, high // tiles), lambda i: (0, i))
        right_spec = pl.BlockSpec((rows, wide), lambda i: (0, 0))
        out_spec = pl.BlockSpec(block, lambda i: (layer, 0, i, 0))

    def kernel(left_ref, right_ref, *refs):
        out = refs[-1]
        value = right_ref[...].reshape(rows, wide)
        total = lax.dot_general(
            left_ref[...], value, (((0,), (0,)), ((), ())), preferred_element_type=f32
        )
        out[...] = total.astype(bf16).reshape(out.shape)

    arrays, specs, aliases = [left, right], [left_spec, right_spec], {}
    if buffer is not None:
        arrays, specs, aliases = arrays + [buffer], specs + [pl.BlockSpec(memory_space=pl.ANY)], {2: 0}
    return pl.pallas_call(
        kernel,
        grid=(tiles,),
        in_specs=specs,
        out_specs=out_spec,
        out_shape=jax.ShapeDtypeStruct(shape, bf16),
        input_output_aliases=aliases,
        compiler_params=pltpu.CompilerParams(vmem_limit_bytes=48 * 1024 * 1024),
        cost_estimate=pl.CostEstimate(
            flops=2 * right.size * high,
            bytes_accessed=2 * (left.size + right.size) + 2 * tiles * high * wide,
            transcendentals=0,
        ),
    )(*arrays)


def row_target(route_rows, place_row, capacity):
    experts = lax.axis_size("ep")
    expert_ids = jnp.arange(experts, dtype=jnp.int32)
    expert_hit = route_rows[:, 0][:, None] == expert_ids[None, :]
    dest_slot = jnp.sum(jnp.where(expert_hit, place_row[None, :], 0), axis=1)
    slot_hit = (dest_slot[:, None] == expert_ids[None, :]).astype(jnp.int32)
    slot_rank = jnp.sum(jnp.cumsum(slot_hit, axis=0) * slot_hit, axis=1) - 1
    return dest_slot * (lax.axis_size("grp") * capacity) + slot_rank


def inverse_of(activation):
    widened = activation.astype(f32)
    return lax.rsqrt(jnp.mean(widened * widened, axis=-1) + 1e-06)


def picker_of(target, row_total):
    return (jnp.arange(row_total, dtype=jnp.int32)[:, None] == target[None, :]).astype(bf16)


def pick(picker, rows):
    return jnp.dot(picker, rows, preferred_element_type=f32).astype(bf16)


def unpick(picker, rows):
    return lax.dot_general(picker, rows, (((0,), (0,)), ((), ())), preferred_element_type=f32)


def below(grad_above, inverse, unit_feat, returned, gain_row):
    width = unit_feat.shape[1]
    d_scaled = returned[:, :width] * gain_row
    first = width + DOTS
    mean = (returned[:, first : first + 1] + returned[:, first + 1 : first + 2]) / (
        lax.axis_size("grp") * width
    )
    return (grad_above.astype(f32) + inverse * (d_scaled - unit_feat * mean)).astype(bf16)


def body(layer_input, middle, upstream, gains, routes, gates, placement, in_proj, out_proj):
    groups = lax.axis_size("grp")
    experts = lax.axis_size("ep")
    here = lax.axis_index("grp")
    tokens = middle.shape[0]
    width = middle.shape[1] // groups
    capacity = 3 * tokens // (2 * experts)
    row_total = groups * experts * capacity
    gain_block = block_of(gains, here, width, 1)

    middle_blocks = feature_blocks(middle)
    middle_slots = send_blocks(middle_blocks)
    middle_t = jnp.stack(middle_slots).reshape(-1, width)
    small = jnp.stack(
        [
            inverse_of(layer_input),
            inverse_of(middle),
            gates[0, :, 0],
            gates[1, :, 0],
            row_target(routes[0], placement[0], capacity).astype(f32),
            row_target(routes[1], placement[1], capacity).astype(f32),
        ]
    )
    small_t = spread_small(after(small, middle_slots[1]))
    inverse = [small_t[:, j].reshape(-1, 1) for j in range(2)]
    gate = [small_t[:, 2 + j].reshape(-1, 1) for j in range(2)]
    ranks = ((here - jnp.arange(groups, dtype=jnp.int32)) % groups * capacity)[:, None]
    picker = [
        picker_of((small_t[:, 4 + j].astype(jnp.int32) + ranks).reshape(-1), row_total)
        for j in range(2)
    ]

    unit_1 = middle_t.astype(f32) * inverse[1]
    features_1 = to_experts(pick(picker[1], (unit_1 * gain_block[1]).astype(bf16)))
    both = feature_blocks(after(jnp.concatenate([upstream, layer_input]), middle_slots[1]))
    both = jnp.stack(send_blocks(both)).reshape(groups, 2, tokens, width)
    upstream_t, input_t = (both[:, part].reshape(-1, width) for part in range(2))
    scaled_1 = (gate[1] * upstream_t.astype(f32)).astype(bf16)
    up_rows_1 = to_experts(pick(picker[1], scaled_1))
    unit_0 = input_t.astype(f32) * inverse[0]

    pre = pre_parts(features_1, in_proj, 1, 2)
    up_rows_1 = to_experts(pick(picker[1], scaled_1))
    pre, _ = scatter_halves(pre)
    back = back_parts(up_rows_1, out_proj, 1)
    features_0 = to_experts(
        pick(after(picker[0], back[0][0]), (unit_0 * gain_block[0]).astype(bf16))
    )
    back, _ = scatter_halves(back)
    packed, hidden_1 = quarter_grads(pre, back)
    pre_0 = flat(pre_parts(after(features_0, packed[0]), in_proj, 0, 1))
    packed = gather_halves(*packed)
    pre_0, packed = lax.optimization_barrier((pre_0, packed))
    d_rows, grads_1 = rows_from_grads(packed, in_proj, 1, features_1)
    pre_0 = sum_whole(send_chunks(pre_0))
    raw_1 = to_experts(d_rows)
    returned = unpick(picker[1], raw_1)

    pre = gather_halves(*pre_0)
    grad_mid = below(upstream_t, inverse[1], unit_1, returned, gain_block[1])
    scaled_0 = (gate[0] * grad_mid.astype(f32)).astype(bf16)
    up_rows_0 = to_experts(pick(picker[0], scaled_0))
    back = back_parts(up_rows_0, out_proj, 0)
    grads_1 = after(grads_1, back[0][0])
    grad_in_proj = outer_into(None, 1, features_1, grads_1, 2)
    pre, back = lax.optimization_barrier((pre, back))
    hidden_0 = hidden_from_sums(pre)
    grad_out_proj = outer_into(None, 0, hidden_0, up_rows_0, 2)
    back = gather_halves(*sum_parts(scatter_halves(back)[0]))
    back, grad_in_proj, grad_out_proj = lax.optimization_barrier(
        (back, grad_in_proj, grad_out_proj)
    )
    d_rows, grads = rows_from_sums(pre, back, in_proj, 0, features_0)
    raw_0 = to_experts(d_rows)
    hidden_1 = join_rows(gather_halves(*after(tuple(hidden_1), d_rows)))
    grad_in_proj = outer_into(grad_in_proj, 0, features_0, grads, 2)
    grad_out_proj = outer_into(grad_out_proj, 1, hidden_1, up_rows_1, 2)
    picker_0, grad_in_proj, grad_out_proj = lax.optimization_barrier(
        (picker[0], grad_in_proj, grad_out_proj)
    )
    returned = unpick(picker_0, raw_0)
    grad_low = below(grad_mid, inverse[0], unit_0, returned, gain_block[0])
    grad_input, first_piece = join_features(grad_low)
    raw_0 = after(raw_0, first_piece)
    gain_sum = jnp.stack([gain_of(raw_0, width), gain_of(raw_1, width)]) / gain_block

    grad_gains = jnp.zeros(gains.shape, f32)
    for step in range(groups):
        piece = gain_sum if step == 0 else shift_grp(gain_sum, step)
        grad_gains = lax.dynamic_update_slice(
            grad_gains, piece, (0, (here - step) % groups * width)
        )

    return (grad_input, grad_in_proj, grad_out_proj, grad_gains)


def solution(mesh):
    return jax.shard_map(
        body,
        mesh=mesh,
        in_specs=(
            P(("grp", "ep"), None),
            P(("grp", "ep"), None),
            P(("grp", "ep"), None),
            P(),
            P(None, ("grp", "ep"), None),
            P(None, ("grp", "ep"), None),
            P(),
            P(None, "ep", None, "grp", None),
            P(None, "ep", None, "grp"),
        ),
        out_specs=(
            P(("grp", "ep"), None),
            P(None, "ep", None, "grp", None),
            P(None, "ep", None, "grp"),
            P(),
        ),
        check_vma=False,
    )
```
